128 devices in a mesh: row: 8 (over x_hi, y), col: 16 (over z, x_lo, core).
Axes of the slice: x: 4 (x_hi: 2, x_lo: 2; x = x_hi * 2 + x_lo), y: 4, z: 4, core: 2. Of those that a mesh axis runs over, the one named last changes fastest.
Arguments:
- val_band: int32 [2048], P(('row', 'col')), may hold values from 0 to 1023, as said below
- cond_band: int32 [2048], P(('row', 'col')), may hold values from 0 to 1023, as said below
- val_orbitals: bfloat16 [1024, 524288], P(('row', 'col')), may hold values from -6 to 6
- cond_orbitals: bfloat16 [1024, 524288], P(('row', 'col')), may hold values from -6 to 6
- val_energy: float32 [1024], replicated, may hold values from -14 to -2
- cond_energy: float32 [1024], replicated, may hold values from 0.5 to 12
- gvec_index: int32 [10240], replicated, may hold values from 0 to 524287, as said below
Outputs:
- chi_real: float32 [10240, 10240], P('row', 'col')
- chi_imag: float32 [10240, 10240], P('row', 'col')
The draws below stay inside these ranges and needn't reach their ends.
Inputs may be any that keep to these rules, and one draw needn't show every extreme that they name: `val_band`: pair p's valence band lies in the block of 8 bands that starts at (p // 16) * 8. `cond_band`: pair p's conduction band lies in the block of 8 bands that starts at (p // 16) * 8. `gvec_index`: all entries differ; each is (kx * 64 + ky) * 128 + kz with kx in 0 to 15 or 48 to 63, ky in 0 to 15 or 48 to 63, and kz in 0 to 31 or 96 to 127.
All inputs are finite; a program needn't handle non-finite values.
Results may differ from the reference program's by a relative error of at most 0.0041.
Values may be sent and summed in bfloat16 or wider, within the bound.
No kernel may reach another device: no remote copies, remote signals or barrier semaphores. Data moves between devices by JAX's collectives and lax.ppermute only.
A program may use at most 192 MiB of HBM per device.

```python
import math
import jax
import jax.numpy as jnp
from jax import lax

GX = 64
GY = 64
GZ = 128
HX = 16
HZ = 32
NR = 524288
NG = 10240
VAL_DEV = 8
COND_DEV = 8
NV = 1024
NC = 1024
PAIR_DEV = 16
PAIRS = 2048


def owned_bands(key, per_block):
    local = jax.random.randint(key, (PAIRS,), 0, per_block).astype(jnp.int32)
    local = local.at[0].set(0).at[PAIRS - 1].set(per_block - 1)
    owner = jnp.arange(PAIRS, dtype=jnp.int32) // PAIR_DEV
    return (owner * per_block + local).astype(jnp.int32)


def draw_val_band(key, part):
    key = jax.random.fold_in(key, 11)
    return owned_bands(key, VAL_DEV)


def draw_cond_band(key, part):
    key = jax.random.fold_in(key, 13)
    return owned_bands(key, COND_DEV)


def draw_gvec_index(key, part):
    key = jax.random.fold_in(key, 7)
    first_key, second_key = jax.random.split(key)
    box_total = 8 * HX * HX * HZ
    others = 1 + jax.random.permutation(first_key, box_total - 2)[:NG - 2]
    ends = jnp.array([0, box_total - 1], dtype=jnp.int32)
    joined = jnp.concatenate([ends, others.astype(jnp.int32)])
    order = jax.random.permutation(second_key, NG)
    boxed = joined[order].astype(jnp.int32)
    box_x = boxed // (4 * HX * HZ)
    box_y = boxed // (2 * HZ) % (2 * HX)
    box_z = boxed % (2 * HZ)
    grid_x = jnp.where(box_x < HX, box_x, box_x + GX - 2 * HX)
    grid_y = jnp.where(box_y < HX, box_y, box_y + GY - 2 * HX)
    grid_z = jnp.where(box_z < HZ, box_z, box_z + GZ - 2 * HZ)
    return ((grid_x * GY + grid_y) * GZ + grid_z).astype(jnp.int32)


def level_of(rng, shape, cuts, least, top_value):
    gain = 1.0
    for position, parts in cuts:
        draws = jax.random.uniform(jax.random.fold_in(jax.random.fold_in(rng, 6), position), (parts,), jnp.float32, least / len(cuts), top_value / len(cuts))
        gain = gain * jnp.repeat(jnp.exp(draws), shape[position] // parts).reshape((-1,) + (1,) * (len(shape) - 1 - position))
    return gain


def normal_values(rng, extent, deviation, limit, pieces=(), held_as=jnp.bfloat16):
    entries = jax.random.normal(rng, extent, jnp.float32) * deviation
    if len(pieces) > 0:
        entries = level_of(rng, extent, pieces, -0.22, 0.18) * entries
    return jnp.clip(entries, min=-limit, max=limit).astype(held_as)


def setup_inputs(seed: int = 0) -> dict:
    keys = jax.random.split(jax.random.key(seed), 8)
    val_band = draw_val_band(jax.random.fold_in(keys[7], 71), 0)
    cond_band = draw_cond_band(jax.random.fold_in(keys[7], 71), 0)
    val_orbitals = normal_values(keys[2], (NV, NR), 1.0, 6.0, ((0, 128),))
    cond_orbitals = normal_values(keys[3], (NC, NR), 1.0, 6.0, ((0, 128),))
    val_energy = jnp.clip(jax.random.uniform(keys[4], (NV,), jnp.float32, -14.0, -2.0), -14.0, -2.0)
    cond_energy = jnp.clip(jax.random.uniform(keys[5], (NC,), jnp.float32, 0.5, 12.0), 0.5, 12.0)
    gvec_index = draw_gvec_index(jax.random.fold_in(keys[7], 71), 0)
    return {"val_band": val_band, "cond_band": cond_band, "val_orbitals": val_orbitals, "cond_orbitals": cond_orbitals, "val_energy": val_energy, "cond_energy": cond_energy, "gvec_index": gvec_index}


def reference(val_band, cond_band, val_orbitals, cond_orbitals, val_energy, cond_energy, gvec_index):
    inv_root = 1.0 / math.sqrt(NR)
    block_size = math.gcd(PAIRS, 16)

    def one_block(indices):
        val_rows, cond_rows = indices
        density = val_orbitals[val_rows].astype(jnp.float32) * cond_orbitals[cond_rows].astype(jnp.float32)
        spectrum = jnp.fft.fftn(density.reshape(-1, GX, GY, GZ), axes=(1, 2, 3)).reshape(-1, NR)
        picked = spectrum[:, gvec_index]
        real_part = jnp.real(picked).astype(jnp.float32) * inv_root
        imag_part = jnp.imag(picked).astype(jnp.float32) * inv_root
        return (real_part, imag_part)
    real_all, imag_all = lax.map(one_block, (val_band.reshape(-1, block_size), cond_band.reshape(-1, block_size)))
    elements = jnp.stack([real_all.reshape(PAIRS, NG), imag_all.reshape(PAIRS, NG)])
    energy_gap = cond_energy[cond_band] - val_energy[val_band]
    factor = -4.0 / (math.sqrt(PAIRS) * energy_gap)
    plain_elems = elements.astype(jnp.bfloat16)
    weighted = (elements * factor[None, :, None]).astype(jnp.bfloat16)
    left_side = plain_elems.reshape(2 * PAIRS, NG)
    right_real = weighted.reshape(2 * PAIRS, NG)
    right_imag = jnp.stack([-weighted[1], weighted[0]]).reshape(2 * PAIRS, NG)
    chi_real = jnp.dot(left_side.T, right_real, preferred_element_type=jnp.float32)
    chi_imag = jnp.dot(left_side.T, right_imag, preferred_element_type=jnp.float32)
    return (chi_real, chi_imag)
```

```python
import functools
import math

import jax
import jax.numpy as jnp
import ml_dtypes
import numpy as np
from jax import lax
from jax.experimental import pallas as pl
from jax.experimental.pallas import tpu as pltpu
from jax.sharding import PartitionSpec as P

GX, GY, GZ = 64, 64, 128
HX, HZ = 16, 32
BANDS = 8
GROUP = 8
NKY = HX + 1
ROWS1 = 40
KXP = 40
OCTS = KXP // 8
KZP = 72
SLOTS = NKY * OCTS + 1
XCH = 8
STEPS = GX // XCH
LANES = 128


def split_table(table):
    hi = table.astype(ml_dtypes.bfloat16)
    lo = (table - hi.astype(np.float64)).astype(ml_dtypes.bfloat16)
    return hi, lo


def tables():
    ky = np.arange(NKY)
    ang = 2.0 * np.pi * ((ky[:, None] * np.arange(GY)[None, :]) % GY) / GY
    first = np.zeros((ROWS1, GY))
    first[:NKY] = np.cos(ang)
    first[NKY : 2 * NKY] = -np.sin(ang)
    hi, lo = split_table(first)
    t1 = np.concatenate(
        [np.concatenate([hi, hi], 1), np.concatenate([lo, np.zeros_like(lo)], 1)], 0
    )
    kx = np.arange(2 * HX + 1) - HX
    ang = 2.0 * np.pi * ((kx[:, None] * np.arange(GX)[None, :]) % GX) / GX
    second = np.zeros((2 * KXP, 2 * GX))
    second[: 2 * HX + 1] = np.concatenate([np.cos(ang), np.sin(ang)], 1)
    second[KXP : KXP + 2 * HX + 1] = np.concatenate([-np.sin(ang), np.cos(ang)], 1)
    hi, lo = split_table(second)
    t2 = np.concatenate(
        [np.concatenate([hi, hi], 1), np.concatenate([lo, np.zeros_like(lo)], 1)], 0
    )
    kz = np.arange(2 * HZ + 1) - HZ
    ang = 2.0 * np.pi * ((kz[:, None] * np.arange(GZ)[None, :]) % GZ) / GZ
    third = np.zeros((2 * KZP, GZ))
    third[: 2 * HZ + 1] = np.cos(ang)
    third[KZP : KZP + 2 * HZ + 1] = np.sin(ang)
    hi, lo = split_table(third)
    t3 = np.concatenate(
        [np.concatenate([hi, hi], 1), np.concatenate([lo, np.zeros_like(lo)], 1)], 0
    )
    perm = np.zeros((LANES, LANES))
    for sub in range(8):
        for rp in range(2 * GROUP):
            perm[sub * 2 * GROUP + rp, rp * 8 + sub] = 1.0
    return t1, t2, t3, perm.astype(ml_dtypes.bfloat16)


def split_value(value):
    hi = value.astype(jnp.bfloat16)
    lo = (value - hi.astype(jnp.float32)).astype(jnp.bfloat16)
    return hi, lo


NN = (((1,), (0,)), ((), ()))
NT = (((1,), (1,)), ((), ()))


def mm(a, b, dims):
    return lax.dot_general(a, b, dims, preferred_element_type=jnp.float32)


def elements_kernel(
    row_blocks,
    col_blocks,
    num_gvec,
    val_rows,
    cond_rows,
    where_row,
    val_ref,
    cond_ref,
    t1_ref,
    t2_ref,
    t3_ref,
    perm_ref,
    scale_ref,
    sub_ref,
    sign_ref,
    rows_ref,
    cols_ref,
    uval,
    ucond,
    first,
    second,
    spectrum,
    picked,
):
    step = pl.program_id(0)

    def unpack(i, carry):
        for j in range(16):
            at = i * 16 + j
            columns = pl.ds(pl.multiple_of(at * LANES, LANES), LANES)
            rows = pl.ds(pl.multiple_of(at * BANDS, BANDS), BANDS)
            uval[rows, :] = val_ref[:, columns].astype(jnp.float32)
            ucond[rows, :] = cond_ref[:, columns].astype(jnp.float32)
        return carry

    lax.fori_loop(0, XCH * GY // 16, unpack, 0)

    def pair_first(p, carry):
        vb = val_rows[p]
        cb = cond_rows[p]
        for half in range(XCH // 2):
            parts = []
            for x in (2 * half, 2 * half + 1):
                base = x * GY * BANDS
                density = (
                    uval[pl.ds(base + vb, GY, stride=BANDS), :]
                    * ucond[pl.ds(base + cb, GY, stride=BANDS), :]
                )
                hi, lo = split_value(density)
                parts.append(jnp.concatenate([hi, lo], axis=0))
            out = mm(t1_ref[...], jnp.concatenate(parts, axis=1), NN)
            out = out[:ROWS1] + out[ROWS1:]
            for k in range(2):
                at = (p * GX + step * XCH + 2 * half + k) * ROWS1
                first[pl.ds(pl.multiple_of(at, 8), ROWS1), :] = out[:, k * LANES : (k + 1) * LANES]
        return carry

    lax.fori_loop(0, GROUP, pair_first, 0)

    @pl.when(step == STEPS - 1)
    def _():
        def second_stage(ky, carry):
            for duo in range(GROUP // 2):
                parts = []
                for p in (2 * duo, 2 * duo + 1):
                    base = p * GX * ROWS1
                    real = first[pl.ds(base + ky, GX, stride=ROWS1), :]
                    imag = first[pl.ds(base + NKY + ky, GX, stride=ROWS1), :]
                    rhi, rlo = split_value(real)
                    ihi, ilo = split_value(imag)
                    parts.append(jnp.concatenate([rhi, ihi, rlo, ilo], axis=0))
                out = mm(t2_ref[...], jnp.concatenate(parts, axis=1), NN)
                out = out[: 2 * KXP] + out[2 * KXP :]
                for k in range(2):
                    for o in range(OCTS):
                        for ri in range(2):
                            at = (ky * OCTS + o) * LANES + (ri * GROUP + 2 * duo + k) * 8
                            second[pl.ds(pl.multiple_of(at, 8), 8), :] = out[
                                ri * KXP + o * 8 : ri * KXP + o * 8 + 8,
                                k * LANES : (k + 1) * LANES,
                            ]
            return carry

        lax.fori_loop(0, NKY, second_stage, 0)
        second[(SLOTS - 1) * LANES :, :] = jnp.zeros((LANES, LANES), jnp.float32)

        lane = lax.broadcasted_iota(jnp.int32, (1, LANES), 1)
        scale = scale_ref[...]
        swapped = jnp.where(lane < LANES // 2, scale, -scale)

        def third_stage(b, carry):
            value = second[pl.ds(pl.multiple_of(b * 2 * LANES, 2 * LANES), 2 * LANES), :]
            hi, lo = split_value(value)
            out = mm(t3_ref[...], jnp.concatenate([hi, lo], axis=1), NT)
            out = out[: 2 * KZP] + out[2 * KZP :]
            for k in range(2):
                cos_part = out[:KZP, k * LANES : (k + 1) * LANES]
                sin_part = out[KZP:, k * LANES : (k + 1) * LANES]
                done = cos_part * scale + pltpu.roll(sin_part, LANES // 2, 1) * swapped
                at = (2 * b + k) * KZP
                spectrum[pl.ds(pl.multiple_of(at, 8), KZP), :] = done
            return carry

        lax.fori_loop(0, SLOTS // 2, third_stage, 0)

        block = num_gvec // col_blocks
        per_row = col_blocks // row_blocks

        for b in range(col_blocks):

            def pick(i, carry):
                for j in range(16):
                    at = i * 16 + j
                    picked[pl.ds(at, 1), :] = spectrum[pl.ds(where_row[b * block + at], 1), :]
                return carry

            lax.fori_loop(0, block // 16, pick, 0)
            turned = mm(perm_ref[...], picked[...].astype(jnp.bfloat16), NT)
            sub = sub_ref[:, b * block : (b + 1) * block]
            total = jnp.zeros((2 * GROUP, block), jnp.float32)
            for s in range(8):
                total = jnp.where(sub == s, turned[s * 2 * GROUP : (s + 1) * 2 * GROUP], total)
            sign = sign_ref[:, b * block : (b + 1) * block]
            total = jnp.concatenate([total[:GROUP], total[GROUP:] * sign], axis=0)
            total = total.astype(jnp.bfloat16)
            cols_ref[b] = total
            rows_ref[b // per_row, :, (b % per_row) * block : (b % per_row + 1) * block] = total


def pair_elements(val_rows, cond_rows, scale, val, cond, gvec, row_blocks, col_blocks):
    num_gvec = gvec.shape[0]
    kx = gvec // (GY * GZ)
    ky = gvec // GZ % GY
    kz = gvec % GZ
    kx = jnp.where(kx < GX // 2, kx, kx - GX)
    ky = jnp.where(ky < GY // 2, ky, ky - GY)
    kz = jnp.where(kz < GZ // 2, kz, kz - GZ)
    flip = jnp.where(ky < 0, -1, 1)
    kx, ky, kz = kx * flip + HX, ky * flip, kz * flip + HZ
    where_row = (ky * OCTS + kx // 8) * KZP + kz
    sub = (kx % 8)[None, :]
    sign = flip.astype(jnp.float32)[None, :]
    lanes = jnp.tile(jnp.repeat(scale, 8), 2)[None, :]
    t1, t2, t3, perm = tables()
    whole = lambda shape: pl.BlockSpec(shape, lambda i, *_: (0,) * len(shape))
    width = XCH * GY * GZ
    outs = [
        jax.ShapeDtypeStruct((row_blocks, 2 * GROUP, num_gvec // row_blocks), jnp.bfloat16),
        jax.ShapeDtypeStruct((col_blocks, 2 * GROUP, num_gvec // col_blocks), jnp.bfloat16),
    ]
    return pl.pallas_call(
        functools.partial(elements_kernel, row_blocks, col_blocks, num_gvec),
        out_shape=outs,
        grid_spec=pltpu.PrefetchScalarGridSpec(
            num_scalar_prefetch=3,
            grid=(STEPS,),
            in_specs=[
                pl.BlockSpec((BANDS, width), lambda i, *_: (0, i)),
                pl.BlockSpec((BANDS, width), lambda i, *_: (0, i)),
                whole(t1.shape),
                whole(t2.shape),
                whole(t3.shape),
                whole(perm.shape),
                whole((1, LANES)),
                whole((1, num_gvec)),
                whole((1, num_gvec)),
            ],
            out_specs=[whole(o.shape) for o in outs],
            scratch_shapes=[
                pltpu.VMEM((XCH * GY * BANDS, LANES), jnp.float32),
                pltpu.VMEM((XCH * GY * BANDS, LANES), jnp.float32),
                pltpu.VMEM((GROUP * GX * ROWS1, LANES), jnp.float32),
                pltpu.VMEM((SLOTS * LANES, LANES), jnp.float32),
                pltpu.VMEM((SLOTS * KZP, LANES), jnp.float32),
                pltpu.VMEM((num_gvec // col_blocks, LANES), jnp.float32),
            ],
        ),
        compiler_params=pltpu.CompilerParams(vmem_limit_bytes=56 * 1024 * 1024),
    )(val_rows, cond_rows, where_row, val, cond, t1, t2, t3, perm, lanes, sub, sign)


def pick_values(indices, values):
    match = indices[:, None] == jnp.arange(values.shape[0], dtype=jnp.int32)[None, :]
    return jnp.sum(jnp.where(match, values[None, :], 0.0), axis=1)


def local(val_band, cond_band, val_orbitals, cond_orbitals, val_energy, cond_energy, gvec_index):
    row_count = lax.axis_size("row")
    col_count = lax.axis_size("col")
    pair_dev = val_band.shape[0]
    pairs_all = pair_dev * row_count * col_count
    energy_gap = pick_values(cond_band, cond_energy) - pick_values(val_band, val_energy)
    factor = 4.0 / (math.sqrt(pairs_all) * energy_gap)
    scale = jnp.sqrt(factor) / math.sqrt(GX * GY * GZ)
    val_rows = val_band % val_orbitals.shape[0]
    cond_rows = cond_band % cond_orbitals.shape[0]
    left, right = [], []
    for start in range(0, pair_dev, GROUP):
        part = slice(start, start + GROUP)
        rows_part, cols_part = pair_elements(
            val_rows[part],
            cond_rows[part],
            scale[part],
            val_orbitals,
            cond_orbitals,
            gvec_index,
            row_count,
            col_count,
        )
        rows_recv = lax.all_to_all(rows_part, "row", split_axis=0, concat_axis=0, tiled=True)
        cols_recv = lax.all_to_all(cols_part, "col", split_axis=0, concat_axis=0, tiled=True)
        left.append(lax.all_gather(rows_recv, "col", axis=0, tiled=True))
        right.append(lax.all_gather(cols_recv, "row", axis=0, tiled=True))
    real = imag = 0.0
    dims = (((0,), (0,)), ((), ()))
    for lhs, rhs in zip(left, right):
        lhs = lhs.reshape(-1, lhs.shape[-1])
        rhs = rhs.reshape(row_count, col_count, 2, GROUP, -1).transpose(1, 0, 2, 3, 4)
        flipped = jnp.stack([rhs[:, :, 1], -rhs[:, :, 0]], axis=2)
        rhs = -rhs.reshape(lhs.shape[0], -1)
        flipped = flipped.reshape(lhs.shape[0], -1)
        real = real + lax.dot_general(lhs, rhs, dims, preferred_element_type=jnp.float32)
        imag = imag + lax.dot_general(lhs, flipped, dims, preferred_element_type=jnp.float32)
    return (real, imag)


def solution(mesh):
    return jax.shard_map(
        local,
        mesh=mesh,
        in_specs=(
            P(("row", "col")),
            P(("row", "col")),
            P(("row", "col"), None),
            P(("row", "col"), None),
            P(),
            P(),
            P(),
        ),
        out_specs=(P("row", "col"), P("row", "col")),
        check_vma=False,
    )
```

```python
import functools
import math

import jax
import jax.numpy as jnp
import ml_dtypes
import numpy as np
from jax import lax
from jax.experimental import pallas as pl
from jax.experimental.pallas import tpu as pltpu
from jax.sharding import PartitionSpec as P

GX, GY, GZ = 64, 64, 128
HX, HZ = 16, 32
BANDS = 8
GROUP = 8
GROUPS = 2
PAIR_DEV = GROUP * GROUPS
NKY = HX + 1
ROWS1 = 40
KXP = 40
OCTS = KXP // 8
KZP = 40
SLOTS = NKY * OCTS
XCH = 8
STEPS = GX // XCH
SPAN = XCH * GY + 8
LANES = 128


def split_table(table):
    hi = table.astype(ml_dtypes.bfloat16)
    lo = (table - hi.astype(np.float64)).astype(ml_dtypes.bfloat16)
    return hi, lo


def tables():
    ky = np.arange(NKY)
    ang = 2.0 * np.pi * ((ky[:, None] * np.arange(GY)[None, :]) % GY) / GY
    first = np.zeros((ROWS1, GY))
    first[:NKY] = np.cos(ang)
    first[NKY : 2 * NKY] = -np.sin(ang)
    hi, lo = split_table(first)
    t1 = np.concatenate(
        [np.concatenate([hi, hi], 1), np.concatenate([lo, np.zeros_like(lo)], 1)], 0
    )
    kx = np.arange(2 * HX + 1) - HX
    ang = 2.0 * np.pi * ((kx[:, None] * np.arange(GX)[None, :]) % GX) / GX
    second = np.zeros((2 * KXP, 2 * GX))
    second[: 2 * HX + 1] = np.concatenate([np.cos(ang), np.sin(ang)], 1)
    second[KXP : KXP + 2 * HX + 1] = np.concatenate([-np.sin(ang), np.cos(ang)], 1)
    hi, lo = split_table(second)
    t2 = np.concatenate(
        [np.concatenate([hi, hi], 1), np.concatenate([lo, np.zeros_like(lo)], 1)], 0
    )
    kz = np.arange(HZ + 1)
    ang = 2.0 * np.pi * ((kz[:, None] * np.arange(GZ)[None, :]) % GZ) / GZ
    third = np.zeros((2 * KZP, GZ))
    third[: HZ + 1] = np.cos(ang)
    third[KZP : KZP + HZ + 1] = np.sin(ang)
    hi, lo = split_table(third)
    t3 = np.concatenate(
        [np.concatenate([hi, hi], 1), np.concatenate([lo, np.zeros_like(lo)], 1)], 0
    )
    perm = np.zeros((LANES, LANES))
    for sub in range(8):
        for rp in range(2 * GROUP):
            perm[sub * 2 * GROUP + rp, rp * 8 + sub] = 1.0
    return t1, t2, t3, perm.astype(ml_dtypes.bfloat16)


def split_value(value):
    hi = value.astype(jnp.bfloat16)
    lo = (value - hi.astype(jnp.float32)).astype(jnp.bfloat16)
    return hi, lo


NN = (((1,), (0,)), ((), ()))
NT = (((1,), (1,)), ((), ()))


def mm(a, b, dims):
    return lax.dot_general(a, b, dims, preferred_element_type=jnp.float32)


def elements_kernel(
    row_blocks,
    col_blocks,
    num_gvec,
    val_rows,
    cond_rows,
    where_row,
    val_ref,
    cond_ref,
    t1_ref,
    t2_ref,
    t3_ref,
    perm_ref,
    scale_ref,
    sub_ref,
    sign_ref,
    rows_ref,
    cols_ref,
    uval,
    ucond,
    first,
    second,
    spectrum,
    picked,
):
    step = pl.program_id(0)

    def unpack(i, carry):
        for j in range(16):
            at = i * 16 + j
            columns = pl.ds(pl.multiple_of(at * LANES, LANES), LANES)
            rows = pl.ds(at, BANDS, stride=SPAN)
            uval[rows, :] = val_ref[:, columns].astype(jnp.float32)
            ucond[rows, :] = cond_ref[:, columns].astype(jnp.float32)
        return carry

    lax.fori_loop(0, XCH * GY // 16, unpack, 0)

    def pair_first(p, carry):
        vb = val_rows[p]
        cb = cond_rows[p]
        for half in range(XCH // 2):
            parts = []
            for x in (2 * half, 2 * half + 1):
                base = x * GY
                density = (
                    uval[pl.ds(pl.multiple_of(vb * SPAN + base, 8), GY), :]
                    * ucond[pl.ds(pl.multiple_of(cb * SPAN + base, 8), GY), :]
                )
                hi, lo = split_value(density)
                parts.append(jnp.concatenate([hi, lo], axis=0))
            out = mm(t1_ref[...], jnp.concatenate(parts, axis=1), NN)
            out = out[:ROWS1] + out[ROWS1:]
            for k in range(2):
                at = (p * GX + step * XCH + 2 * half + k) * ROWS1
                first[pl.ds(pl.multiple_of(at, 8), ROWS1), :] = out[:, k * LANES : (k + 1) * LANES]
        return carry

    lax.fori_loop(0, PAIR_DEV, pair_first, 0, unroll=2)

    @pl.when(step == STEPS - 1)
    def _():
        def second_stage(ky, carry):
            for duo in range(PAIR_DEV // 2):
                parts = []
                for p in (2 * duo, 2 * duo + 1):
                    base = p * GX * ROWS1
                    real = first[pl.ds(base + ky, GX, stride=ROWS1), :]
                    imag = first[pl.ds(base + NKY + ky, GX, stride=ROWS1), :]
                    rhi, rlo = split_value(real)
                    ihi, ilo = split_value(imag)
                    parts.append(jnp.concatenate([rhi, ihi, rlo, ilo], axis=0))
                out = mm(t2_ref[...], jnp.concatenate(parts, axis=1), NN)
                out = out[: 2 * KXP] + out[2 * KXP :]
                for k in range(2):
                    for o in range(OCTS):
                        for ri in range(2):
                            group, p = divmod(2 * duo + k, GROUP)
                            at = (ky * OCTS + o) * GROUPS + group
                            at = at * LANES + (ri * GROUP + p) * 8
                            second[pl.ds(pl.multiple_of(at, 8), 8), :] = out[
                                ri * KXP + o * 8 : ri * KXP + o * 8 + 8,
                                k * LANES : (k + 1) * LANES,
                            ]
            return carry

        lax.fori_loop(0, NKY, second_stage, 0)

        lane = lax.broadcasted_iota(jnp.int32, (1, GROUPS * LANES), 1) % LANES
        scale = scale_ref[...]
        swapped = jnp.where(lane < LANES // 2, scale, -scale)

        def third_stage(b, carry):
            value = second[pl.ds(pl.multiple_of(b * 2 * LANES, 2 * LANES), 2 * LANES), :]
            hi, lo = split_value(value)
            out = mm(t3_ref[...], jnp.concatenate([hi, lo], axis=1), NT)
            out = out[: 2 * KZP] + out[2 * KZP :]
            cos_part = out[:KZP] * scale
            sin_part = jnp.concatenate(
                [
                    pltpu.roll(out[KZP:, k * LANES : (k + 1) * LANES], LANES // 2, 1)
                    for k in range(GROUPS)
                ],
                axis=1,
            )
            sin_part = sin_part * swapped
            at = b * 2 * KZP
            plus = cos_part + sin_part
            minus = cos_part - sin_part
            for k in range(GROUPS):
                part = slice(k * LANES, (k + 1) * LANES)
                spectrum[k, pl.ds(pl.multiple_of(at, 8), KZP), :] = plus[:, part]
                spectrum[k, pl.ds(pl.multiple_of(at + KZP, 8), KZP), :] = minus[:, part]
            return carry

        lax.fori_loop(0, SLOTS, third_stage, 0, unroll=5)

        block = num_gvec // col_blocks
        per_row = col_blocks // row_blocks

        for b in range(col_blocks):

            def pick(i, carry):
                for j in range(64):
                    at = i * 64 + j
                    row = where_row[b * block + at]
                    for k in range(GROUPS):
                        picked[k, pl.ds(at, 1), :] = spectrum[k, pl.ds(row, 1), :]
                return carry

            lax.fori_loop(0, block // 64, pick, 0)
            sub = sub_ref[:, b * block : (b + 1) * block]
            sign = sign_ref[:, b * block : (b + 1) * block]
            real, imag = [], []
            for k in range(GROUPS):
                part = picked[k].astype(jnp.bfloat16)
                turned = mm(perm_ref[...], part, NT)
                total = turned[: 2 * GROUP]
                for s in range(1, 8):
                    total = jnp.where(sub == s, turned[s * 2 * GROUP : (s + 1) * 2 * GROUP], total)
                real.append(total[:GROUP])
                imag.append(total[GROUP:] * sign)
            total = jnp.concatenate(real + imag, axis=0).astype(jnp.bfloat16)
            cols_ref[b] = total
            rows_ref[b // per_row, :, (b % per_row) * block : (b % per_row + 1) * block] = total


def pair_elements(val_rows, cond_rows, scale, val, cond, gvec, row_blocks, col_blocks):
    num_gvec = gvec.shape[0]
    kx = gvec // (GY * GZ)
    ky = gvec // GZ % GY
    kz = gvec % GZ
    kx = jnp.where(kx < GX // 2, kx, kx - GX)
    ky = jnp.where(ky < GY // 2, ky, ky - GY)
    kz = jnp.where(kz < GZ // 2, kz, kz - GZ)
    flip = jnp.where(ky < 0, -1, 1)
    kx, ky, kz = kx * flip + HX, ky * flip, kz * flip
    where_row = (ky * OCTS + kx // 8) * 2 * KZP + jnp.where(kz < 0, KZP - kz, kz)
    sub = (kx % 8)[None, :]
    sign = flip.astype(jnp.float32)[None, :]
    lanes = jnp.repeat(scale, 8).reshape(GROUPS, 1, -1)
    lanes = jnp.tile(lanes, (1, 2, 1)).reshape(1, -1)
    t1, t2, t3, perm = tables()
    whole = lambda shape: pl.BlockSpec(shape, lambda i, *_: (0,) * len(shape))
    width = XCH * GY * GZ
    outs = [
        jax.ShapeDtypeStruct((row_blocks, 2 * PAIR_DEV, num_gvec // row_blocks), jnp.bfloat16),
        jax.ShapeDtypeStruct((col_blocks, 2 * PAIR_DEV, num_gvec // col_blocks), jnp.bfloat16),
    ]
    return pl.pallas_call(
        functools.partial(elements_kernel, row_blocks, col_blocks, num_gvec),
        out_shape=outs,
        grid_spec=pltpu.PrefetchScalarGridSpec(
            num_scalar_prefetch=3,
            grid=(STEPS,),
            in_specs=[
                pl.BlockSpec((BANDS, width), lambda i, *_: (0, i)),
                pl.BlockSpec((BANDS, width), lambda i, *_: (0, i)),
                whole(t1.shape),
                whole(t2.shape),
                whole(t3.shape),
                whole(perm.shape),
                whole((1, GROUPS * LANES)),
                whole((1, num_gvec)),
                whole((1, num_gvec)),
            ],
            out_specs=[whole(o.shape) for o in outs],
            scratch_shapes=[
                pltpu.VMEM((SPAN * BANDS, LANES), jnp.float32),
                pltpu.VMEM((SPAN * BANDS, LANES), jnp.float32),
                pltpu.VMEM((PAIR_DEV * GX * ROWS1, LANES), jnp.float32),
                pltpu.VMEM((SLOTS * GROUPS * LANES, LANES), jnp.float32),
                pltpu.VMEM((GROUPS, SLOTS * 2 * KZP, LANES), jnp.float32),
                pltpu.VMEM((GROUPS, num_gvec // col_blocks, LANES), jnp.float32),
            ],
        ),
        compiler_params=pltpu.CompilerParams(vmem_limit_bytes=60 * 1024 * 1024),
    )(val_rows, cond_rows, where_row, val, cond, t1, t2, t3, perm, lanes, sub, sign)


def product_kernel(chunk_row, chunk_col, *refs):
    lefts = refs[: len(LEFT)]
    rights = refs[len(LEFT) : len(LEFT) + len(RIGHT)]
    real_ref, imag_ref, table = refs[len(LEFT) + len(RIGHT) :]
    width = rights[0].shape[2]
    rows = 2 * PAIR_DEV

    @pl.when(pl.program_id(0) == 0)
    def _():
        def fill(i, carry):
            for k, right in enumerate(rights):
                value = right[chunk_col[i]]
                at = (i * len(RIGHT) + chunk_row[k]) * rows
                first = pl.ds(pl.multiple_of(at, rows), PAIR_DEV)
                last = pl.ds(pl.multiple_of(at + PAIR_DEV, PAIR_DEV), PAIR_DEV)
                table[first, :width] = -value[:PAIR_DEV]
                table[last, :width] = -value[PAIR_DEV:]
                table[first, width:] = value[PAIR_DEV:]
                table[last, width:] = -value[:PAIR_DEV]
            return carry

        lax.fori_loop(0, len(LEFT), fill, 0)

    left = jnp.concatenate([ref[...].reshape(-1, ref.shape[2]) for ref in lefts], axis=0)
    out = mm(left, table[...], (((0,), (0,)), ((), ())))
    real_ref[...] = out[:, :width]
    imag_ref[...] = out[:, width:]


HALF = [(0, 0), (0, 1), (-1, 0), (1, 0), (-1, 1), (1, 1), (2, 0), (2, 1)]
LEFT = [(dz, dx, core) for core in range(2) for dz, dx in HALF]
RIGHT = [(dx, dy) for dy, dx in HALF]
TILE = 256


def panel_product(lefts, rights):
    row, col = lax.axis_index("row"), lax.axis_index("col")
    chunk_col = jnp.stack(
        [(col // 4 + dz) % 4 * 4 + (col // 2 % 2 ^ dx) * 2 + (col % 2 ^ dc) for dz, dx, dc in LEFT]
    )
    chunk_row = jnp.stack([(row // 4 ^ dx) * 4 + (row % 4 + dy) % 4 for dx, dy in RIGHT])
    sources, rows, height = lefts[0].shape
    width = rights[0].shape[2]
    depth = len(lefts) * sources * rows
    out = jax.ShapeDtypeStruct((height, width), jnp.float32)
    return pl.pallas_call(
        product_kernel,
        out_shape=[out, out],
        grid_spec=pltpu.PrefetchScalarGridSpec(
            num_scalar_prefetch=2,
            grid=(height // TILE,),
            in_specs=[pl.BlockSpec((sources, rows, TILE), lambda m, *_: (0, 0, m))] * len(lefts)
            + [pl.BlockSpec(rights[0].shape, lambda m, *_: (0, 0, 0))] * len(rights),
            out_specs=[pl.BlockSpec((TILE, width), lambda m, *_: (m, 0))] * 2,
            scratch_shapes=[pltpu.VMEM((depth, 2 * width), jnp.bfloat16)],
        ),
        compiler_params=pltpu.CompilerParams(vmem_limit_bytes=60 * 1024 * 1024),
    )(chunk_row, chunk_col, *lefts, *rights)


def ring_chunks(own, axis, ring, swap):
    send = lambda value, perm: lax.ppermute(value, axis, perm)
    near = (send(own, ring(1)), send(own, ring(-1)))
    other = send(own, swap)
    far = (send(other, ring(1)), send(other, ring(-1)))
    ends = (send(near[0], ring(1)), send(far[1], ring(-1)))
    return [own, other, *near, *far, *ends]


def ring_z(step):
    return [(c, (c // 4 + step) % 4 * 4 + c % 4) for c in range(16)]


def ring_y(step):
    return [(r, r // 4 * 4 + (r + step) % 4) for r in range(8)]


def pick_values(indices, values):
    match = indices[:, None] == jnp.arange(values.shape[0], dtype=jnp.int32)[None, :]
    return jnp.sum(jnp.where(match, values[None, :], 0.0), axis=1)


def local(val_band, cond_band, val_orbitals, cond_orbitals, val_energy, cond_energy, gvec_index):
    row_count = lax.axis_size("row")
    col_count = lax.axis_size("col")
    pair_dev = val_band.shape[0]
    pairs_all = pair_dev * row_count * col_count
    energy_gap = pick_values(cond_band, cond_energy) - pick_values(val_band, val_energy)
    factor = 4.0 / (math.sqrt(pairs_all) * energy_gap)
    scale = jnp.sqrt(factor) / math.sqrt(GX * GY * GZ)
    val_rows = val_band % val_orbitals.shape[0]
    cond_rows = cond_band % cond_orbitals.shape[0]
    rows_part, cols_part = pair_elements(
        val_rows, cond_rows, scale, val_orbitals, cond_orbitals, gvec_index, row_count, col_count
    )
    rows_recv = lax.all_to_all(rows_part, "row", split_axis=0, concat_axis=0, tiled=True)
    cols_part, rows_recv = lax.optimization_barrier((cols_part, rows_recv))
    lefts = ring_chunks(rows_recv, "col", ring_z, [(c, c ^ 2) for c in range(16)])
    cols_recv = lax.all_to_all(cols_part, "col", split_axis=0, concat_axis=0, tiled=True)
    rights = ring_chunks(cols_recv, "row", ring_y, [(r, r ^ 4) for r in range(8)])
    lefts += [lax.ppermute(left, "col", [(c, c ^ 1) for c in range(16)]) for left in lefts]
    real, imag = panel_product(lefts, rights)
    return (real, imag)


def solution(mesh):
    return jax.shard_map(
        local,
        mesh=mesh,
        in_specs=(
            P(("row", "col")),
            P(("row", "col")),
            P(("row", "col"), None),
            P(("row", "col"), None),
            P(),
            P(),
            P(),
        ),
        out_specs=(P("row", "col"), P("row", "col")),
        check_vma=False,
    )
```

```python
import functools
import math

import jax
import jax.numpy as jnp
import ml_dtypes
import numpy as np
from jax import lax
from jax.experimental import pallas as pl
from jax.experimental.pallas import tpu as pltpu
from jax.sharding import PartitionSpec as P

GX, GY, GZ = 64, 64, 128
HX, HZ = 16, 32
BANDS = 8
GROUP = 8
GROUPS = 2
PAIR_DEV = GROUP * GROUPS
NKY = HX + 1
ROWS1 = 40
KXP = 40
OCTS = KXP // 8
KZP = 40
SLOTS = NKY * OCTS
XCH = 8
STEPS = GX // XCH
SPAN = XCH * GY + 8
LANES = 128


def split_table(table):
    hi = table.astype(ml_dtypes.bfloat16)
    lo = (table - hi.astype(np.float64)).astype(ml_dtypes.bfloat16)
    return hi, lo


def tables():
    ky = np.arange(NKY)
    ang = 2.0 * np.pi * ((ky[:, None] * np.arange(GY)[None, :]) % GY) / GY
    first = np.zeros((ROWS1, GY))
    first[:NKY] = np.cos(ang)
    first[NKY : 2 * NKY] = -np.sin(ang)
    hi, lo = split_table(first)
    t1 = np.concatenate(
        [np.concatenate([hi, hi], 1), np.concatenate([lo, np.zeros_like(lo)], 1)], 0
    )
    kx = np.arange(2 * HX + 1) - HX
    ang = 2.0 * np.pi * ((kx[:, None] * np.arange(GX)[None, :]) % GX) / GX
    second = np.zeros((2 * KXP, 2 * GX))
    second[: 2 * HX + 1] = np.concatenate([np.cos(ang), np.sin(ang)], 1)
    second[KXP : KXP + 2 * HX + 1] = np.concatenate([-np.sin(ang), np.cos(ang)], 1)
    hi, lo = split_table(second)
    t2 = np.concatenate(
        [np.concatenate([hi, hi], 1), np.concatenate([lo, np.zeros_like(lo)], 1)], 0
    )
    kz = np.arange(HZ + 1)
    ang = 2.0 * np.pi * ((kz[:, None] * np.arange(GZ)[None, :]) % GZ) / GZ
    third = np.zeros((2 * KZP, GZ))
    third[: HZ + 1] = np.cos(ang)
    third[KZP : KZP + HZ + 1] = np.sin(ang)
    hi, lo = split_table(third)
    t3 = np.concatenate(
        [np.concatenate([hi, hi], 1), np.concatenate([lo, np.zeros_like(lo)], 1)], 0
    )
    perm = np.zeros((LANES, LANES))
    for sub in range(8):
        for rp in range(2 * GROUP):
            perm[sub * 2 * GROUP + rp, rp * 8 + sub] = 1.0
    return t1, t2, t3, perm.astype(ml_dtypes.bfloat16)


def split_value(value):
    hi = value.astype(jnp.bfloat16)
    lo = (value - hi.astype(jnp.float32)).astype(jnp.bfloat16)
    return hi, lo


NN = (((1,), (0,)), ((), ()))
NT = (((1,), (1,)), ((), ()))


def mm(a, b, dims):
    return lax.dot_general(a, b, dims, preferred_element_type=jnp.float32)


def elements_kernel(
    row_blocks,
    col_blocks,
    num_gvec,
    val_rows,
    cond_rows,
    where_row,
    val_ref,
    cond_ref,
    t1_ref,
    t2_ref,
    t3_ref,
    perm_ref,
    scale_ref,
    gvec_ref,
    rows_ref,
    cols_ref,
    uval,
    ucond,
    first,
    second,
    spectrum,
    picked,
):
    step = pl.program_id(0)

    def unpack(i, carry):
        for j in range(16):
            at = i * 16 + j
            columns = pl.ds(pl.multiple_of(at * LANES, LANES), LANES)
            rows = pl.ds(at, BANDS, stride=SPAN)
            uval[rows, :] = val_ref[:, columns].astype(jnp.float32)
            ucond[rows, :] = cond_ref[:, columns].astype(jnp.float32)
        return carry

    lax.fori_loop(0, XCH * GY // 16, unpack, 0)

    def pair_first(p, carry):
        vb = val_rows[p]
        cb = cond_rows[p]
        for half in range(XCH // 2):
            parts = []
            for x in (2 * half, 2 * half + 1):
                base = x * GY
                density = (
                    uval[pl.ds(pl.multiple_of(vb * SPAN + base, 8), GY), :]
                    * ucond[pl.ds(pl.multiple_of(cb * SPAN + base, 8), GY), :]
                )
                hi, lo = split_value(density)
                parts.append(jnp.concatenate([hi, lo], axis=0))
            out = mm(t1_ref[...], jnp.concatenate(parts, axis=1), NN)
            out = out[:ROWS1] + out[ROWS1:]
            for k in range(2):
                at = (p * GX + step * XCH + 2 * half + k) * ROWS1
                first[pl.ds(pl.multiple_of(at, 8), ROWS1), :] = out[:, k * LANES : (k + 1) * LANES]
        return carry

    lax.fori_loop(0, PAIR_DEV, pair_first, 0, unroll=2)

    @pl.when(step == STEPS - 1)
    def _():
        def second_stage(ky, carry):
            for duo in range(PAIR_DEV // 2):
                parts = []
                for p in (2 * duo, 2 * duo + 1):
                    base = p * GX * ROWS1
                    real = first[pl.ds(base + ky, GX, stride=ROWS1), :]
                    imag = first[pl.ds(base + NKY + ky, GX, stride=ROWS1), :]
                    rhi, rlo = split_value(real)
                    ihi, ilo = split_value(imag)
                    parts.append(jnp.concatenate([rhi, ihi, rlo, ilo], axis=0))
                out = mm(t2_ref[...], jnp.concatenate(parts, axis=1), NN)
                out = out[: 2 * KXP] + out[2 * KXP :]
                for k in range(2):
                    for o in range(OCTS):
                        for ri in range(2):
                            group, p = divmod(2 * duo + k, GROUP)
                            at = (ky * OCTS + o) * GROUPS + group
                            at = at * LANES + (ri * GROUP + p) * 8
                            second[pl.ds(pl.multiple_of(at, 8), 8), :] = out[
                                ri * KXP + o * 8 : ri * KXP + o * 8 + 8,
                                k * LANES : (k + 1) * LANES,
                            ]
            return carry

        lax.fori_loop(0, NKY, second_stage, 0)

        lane = lax.broadcasted_iota(jnp.int32, (1, GROUPS * LANES), 1) % LANES
        scale = scale_ref[...]
        swapped = jnp.where(lane < LANES // 2, scale, -scale)

        def third_stage(b, carry):
            value = second[pl.ds(pl.multiple_of(b * 2 * LANES, 2 * LANES), 2 * LANES), :]
            hi, lo = split_value(value)
            out = mm(t3_ref[...], jnp.concatenate([hi, lo], axis=1), NT)
            out = out[: 2 * KZP] + out[2 * KZP :]
            cos_part = out[:KZP] * scale
            sin_part = jnp.concatenate(
                [
                    pltpu.roll(out[KZP:, k * LANES : (k + 1) * LANES], LANES // 2, 1)
                    for k in range(GROUPS)
                ],
                axis=1,
            )
            sin_part = sin_part * swapped
            at = b * 2 * KZP
            plus = cos_part + sin_part
            minus = cos_part - sin_part
            for k in range(GROUPS):
                part = slice(k * LANES, (k + 1) * LANES)
                spectrum[k, pl.ds(pl.multiple_of(at, 8), KZP), :] = plus[:, part]
                spectrum[k, pl.ds(pl.multiple_of(at + KZP, 8), KZP), :] = minus[:, part]
            return carry

        lax.fori_loop(0, SLOTS, third_stage, 0, unroll=5)

        block = num_gvec // col_blocks
        per_row = col_blocks // row_blocks

        for b in range(col_blocks):

            def pick(i, carry):
                for j in range(64):
                    at = i * 64 + j
                    row = where_row[b * block + at]
                    for k in range(GROUPS):
                        picked[k, pl.ds(at, 1), :] = spectrum[k, pl.ds(row, 1), :]
                return carry

            lax.fori_loop(0, block // 64, pick, 0)
            kx, _, _, flip = signed_parts(gvec_ref[:, b * block : (b + 1) * block])
            sub = kx & 7
            sign = flip.astype(jnp.float32)
            real, imag = [], []
            for k in range(GROUPS):
                part = picked[k].astype(jnp.bfloat16)
                turned = mm(perm_ref[...], part, NT)
                total = turned[: 2 * GROUP]
                for s in range(1, 8):
                    total = jnp.where(sub == s, turned[s * 2 * GROUP : (s + 1) * 2 * GROUP], total)
                real.append(total[:GROUP])
                imag.append(total[GROUP:] * sign)
            total = jnp.concatenate(real + imag, axis=0).astype(jnp.bfloat16)
            cols_ref[b] = total
            rows_ref[b // per_row, :, (b % per_row) * block : (b % per_row + 1) * block] = total


def signed_parts(gvec):
    kx = gvec >> 13
    ky = (gvec >> 7) & (GY - 1)
    kz = gvec & (GZ - 1)
    kx = jnp.where(kx < GX // 2, kx, kx - GX)
    ky = jnp.where(ky < GY // 2, ky, ky - GY)
    kz = jnp.where(kz < GZ // 2, kz, kz - GZ)
    flip = jnp.where(ky < 0, -1, 1)
    return kx * flip + HX, ky * flip, kz * flip, flip


def pair_elements(val_rows, cond_rows, scale, val, cond, gvec, row_blocks, col_blocks):
    num_gvec = gvec.shape[0]
    kx, ky, kz, _ = signed_parts(gvec)
    where_row = (ky * OCTS + (kx >> 3)) * 2 * KZP + jnp.where(kz < 0, KZP - kz, kz)
    lanes = jnp.repeat(scale, 8).reshape(GROUPS, 1, -1)
    lanes = jnp.tile(lanes, (1, 2, 1)).reshape(1, -1)
    t1, t2, t3, perm = tables()
    whole = lambda shape: pl.BlockSpec(shape, lambda i, *_: (0,) * len(shape))
    width = XCH * GY * GZ
    outs = [
        jax.ShapeDtypeStruct((row_blocks, 2 * PAIR_DEV, num_gvec // row_blocks), jnp.bfloat16),
        jax.ShapeDtypeStruct((col_blocks, 2 * PAIR_DEV, num_gvec // col_blocks), jnp.bfloat16),
    ]
    return pl.pallas_call(
        functools.partial(elements_kernel, row_blocks, col_blocks, num_gvec),
        out_shape=outs,
        grid_spec=pltpu.PrefetchScalarGridSpec(
            num_scalar_prefetch=3,
            grid=(STEPS,),
            in_specs=[
                pl.BlockSpec((BANDS, width), lambda i, *_: (0, i)),
                pl.BlockSpec((BANDS, width), lambda i, *_: (0, i)),
                whole(t1.shape),
                whole(t2.shape),
                whole(t3.shape),
                whole(perm.shape),
                whole((1, GROUPS * LANES)),
                whole((1, num_gvec)),
            ],
            out_specs=[whole(o.shape) for o in outs],
            scratch_shapes=[
                pltpu.VMEM((SPAN * BANDS, LANES), jnp.float32),
                pltpu.VMEM((SPAN * BANDS, LANES), jnp.float32),
                pltpu.VMEM((PAIR_DEV * GX * ROWS1, LANES), jnp.float32),
                pltpu.VMEM((SLOTS * GROUPS * LANES, LANES), jnp.float32),
                pltpu.VMEM((GROUPS, SLOTS * 2 * KZP, LANES), jnp.float32),
                pltpu.VMEM((GROUPS, num_gvec // col_blocks, LANES), jnp.float32),
            ],
        ),
        compiler_params=pltpu.CompilerParams(vmem_limit_bytes=60 * 1024 * 1024),
    )(val_rows, cond_rows, where_row, val, cond, t1, t2, t3, perm, lanes, gvec[None, :])


def product_kernel(pairs, chunk_row, chunk_col, *refs):
    lefts, rights, before = refs[: len(LEFT)], refs[len(LEFT) : COUNT], refs[COUNT:-4]
    real_ref, imag_ref, lhs, table = refs[-4:]
    width = rights[0].shape[2]
    rows = 2 * PAIR_DEV

    @pl.when(pl.program_id(0) == 0)
    def _():
        for at, (i, k) in enumerate(pairs):
            value = rights[k][chunk_col[i]]
            first = slice(at * rows, at * rows + PAIR_DEV)
            last = slice(at * rows + PAIR_DEV, (at + 1) * rows)
            table[first, :width] = -value[:PAIR_DEV]
            table[last, :width] = -value[PAIR_DEV:]
            table[first, width:] = value[PAIR_DEV:]
            table[last, width:] = -value[:PAIR_DEV]

    for at, (i, k) in enumerate(pairs):
        lhs[at * rows : (at + 1) * rows, :] = lefts[i][chunk_row[k]]
    out = mm(lhs[...], table[...], (((0,), (0,)), ((), ())))
    real, imag = out[:, :width], out[:, width:]
    if before:
        real += before[0][...]
        imag += before[1][...]
    real_ref[...] = real
    imag_ref[...] = imag


HALF = [(0, 0), (0, 1), (-1, 0), (1, 0), (-1, 1), (1, 1), (2, 0), (2, 1)]
LEFT = [(dz, dx, core) for core in range(2) for dz, dx in HALF]
RIGHT = [(dx, dy) for dy, dx in HALF]
COUNT = len(LEFT) + len(RIGHT)
TILE = 256


def panel_product(lefts, rights, pairs, before=()):
    row, col = lax.axis_index("row"), lax.axis_index("col")
    chunk_col = jnp.stack(
        [(col // 4 + dz) % 4 * 4 + (col // 2 % 2 ^ dx) * 2 + (col % 2 ^ dc) for dz, dx, dc in LEFT]
    )
    chunk_row = jnp.stack([(row // 4 ^ dx) * 4 + (row % 4 + dy) % 4 for dx, dy in RIGHT])
    left_at, right_at = sorted({i for i, _ in pairs}), sorted({k for _, k in pairs})
    sources, rows, height = lefts[0].shape
    width = rights[0].shape[2]
    depth = len(pairs) * rows
    out = jax.ShapeDtypeStruct((height, width), jnp.float32)
    out_spec = pl.BlockSpec((TILE, width), lambda m, *_: (m, 0))

    def kernel(chunk_row, chunk_col, *refs):
        left_refs = dict(zip(left_at, refs))
        refs = refs[len(left_at) :]
        right_refs = dict(zip(right_at, refs))
        refs = refs[len(right_at) :]
        all_left = [left_refs.get(i) for i in range(len(LEFT))]
        all_right = [right_refs.get(k) for k in range(len(RIGHT))]
        product_kernel(pairs, chunk_row, chunk_col, *all_left, *all_right, *refs)

    return pl.pallas_call(
        kernel,
        out_shape=[out, out],
        grid_spec=pltpu.PrefetchScalarGridSpec(
            num_scalar_prefetch=2,
            grid=(height // TILE,),
            in_specs=[pl.BlockSpec((sources, rows, TILE), lambda m, *_: (0, 0, m))] * len(left_at)
            + [pl.BlockSpec(rights[0].shape, lambda m, *_: (0, 0, 0))] * len(right_at)
            + [out_spec] * len(before),
            out_specs=[out_spec] * 2,
            scratch_shapes=[
                pltpu.VMEM((depth, TILE), jnp.bfloat16),
                pltpu.VMEM((depth, 2 * width), jnp.bfloat16),
            ],
        ),
        compiler_params=pltpu.CompilerParams(vmem_limit_bytes=60 * 1024 * 1024),
    )(
        chunk_row,
        chunk_col,
        *[lefts[i] for i in left_at],
        *[rights[k] for k in right_at],
        *before,
    )


def ring_z(step):
    return [(c, (c // 4 + step) % 4 * 4 + c % 4) for c in range(16)]


def ring_y(step):
    return [(r, r // 4 * 4 + (r + step) % 4) for r in range(8)]


def pick_values(indices, values):
    match = indices[:, None] == jnp.arange(values.shape[0], dtype=jnp.int32)[None, :]
    return jnp.sum(jnp.where(match, values[None, :], 0.0), axis=1)


def local(val_band, cond_band, val_orbitals, cond_orbitals, val_energy, cond_energy, gvec_index):
    row_count = lax.axis_size("row")
    col_count = lax.axis_size("col")
    pair_dev = val_band.shape[0]
    pairs_all = pair_dev * row_count * col_count
    energy_gap = pick_values(cond_band, cond_energy) - pick_values(val_band, val_energy)
    factor = 4.0 / (math.sqrt(pairs_all) * energy_gap)
    scale = jnp.sqrt(factor) / math.sqrt(GX * GY * GZ)
    val_rows = val_band % val_orbitals.shape[0]
    cond_rows = cond_band % cond_orbitals.shape[0]
    rows_part, cols_part = pair_elements(
        val_rows, cond_rows, scale, val_orbitals, cond_orbitals, gvec_index, row_count, col_count
    )
    swap_core = [(c, c ^ 1) for c in range(col_count)]
    swap_low = [(c, c ^ 2) for c in range(col_count)]
    swap_high = [(r, r ^ 4) for r in range(row_count)]
    along_z = lambda value, step: lax.ppermute(value, "col", ring_z(step))
    along_y = lambda value, step: lax.ppermute(value, "row", ring_y(step))
    cross = lambda value: lax.ppermute(value, "col", swap_core)
    fence = lax.optimization_barrier

    left = [lax.all_to_all(rows_part, "row", split_axis=0, concat_axis=0, tiled=True)]
    cols_part, left = fence((cols_part, left))
    low = lax.ppermute(left[0], "col", swap_low)
    left_near = [along_z(left[0], 1), along_z(left[0], -1)]
    right = [lax.all_to_all(cols_part, "col", split_axis=0, concat_axis=0, tiled=True)]
    left, right = fence((left + [low] + left_near, right))
    left_far = [along_z(left[1], 1), along_z(left[1], -1)]
    right_near = [along_y(right[0], 1), along_y(right[0], -1)]
    high = lax.ppermute(right[0], "row", swap_high)
    left, right = fence((left + left_far, right + [high] + right_near))
    right_far = [along_y(right[1], 1), along_y(right[1], -1)]
    left_ends = [along_z(left[2], 1), along_z(left[5], -1)]
    crossed = [cross(value) for value in left[:4]]
    left, right, crossed = fence((left + left_ends, right + right_far, crossed))
    right_ends = [along_y(right[2], 1), along_y(right[5], -1)]
    crossed_last = [cross(value) for value in left[4:]]
    early = [(i, k) for i in range(12) for k in range(6)]
    late = [(i, k) for i in range(16) for k in range(8) if (i, k) not in early]
    partial = panel_product(left + crossed, right, early)
    real, imag = panel_product(left + crossed + crossed_last, right + right_ends, late, partial)
    return (real, imag)


def solution(mesh):
    return jax.shard_map(
        local,
        mesh=mesh,
        in_specs=(
            P(("row", "col")),
            P(("row", "col")),
            P(("row", "col"), None),
            P(("row", "col"), None),
            P(),
            P(),
            P(),
        ),
        out_specs=(P("row", "col"), P("row", "col")),
        check_vma=False,
    )
```

```python
import functools
import math

import jax
import jax.numpy as jnp
import ml_dtypes
import numpy as np
from jax import lax
from jax.experimental import pallas as pl
from jax.experimental.pallas import tpu as pltpu
from jax.sharding import PartitionSpec as P

GX, GY, GZ = 64, 64, 128
HX, HZ = 16, 32
BANDS = 8
GROUP = 8
GROUPS = 2
PAIR_DEV = GROUP * GROUPS
NKY = HX + 1
ROWS1 = 40
KXP = 40
OCTS = KXP // 8
KZP = 40
SLOTS = NKY * OCTS
XCH = 16
STEPS = GX // XCH
SPAN = XCH * GY + 8
LANES = 128


def split_table(table):
    hi = table.astype(ml_dtypes.bfloat16)
    lo = (table - hi.astype(np.float64)).astype(ml_dtypes.bfloat16)
    return hi, lo


def tables():
    ky = np.arange(NKY)
    ang = 2.0 * np.pi * ((ky[:, None] * np.arange(GY)[None, :]) % GY) / GY
    first = np.zeros((ROWS1, GY))
    first[:NKY] = np.cos(ang)
    first[NKY : 2 * NKY] = -np.sin(ang)
    hi, lo = split_table(first)
    t1 = np.concatenate(
        [np.concatenate([hi, hi], 1), np.concatenate([lo, np.zeros_like(lo)], 1)], 0
    )
    kx = np.arange(2 * HX + 1) - HX
    ang = 2.0 * np.pi * ((kx[:, None] * np.arange(GX)[None, :]) % GX) / GX
    second = np.zeros((2 * KXP, 2 * GX))
    second[: 2 * HX + 1] = np.concatenate([np.cos(ang), np.sin(ang)], 1)
    second[KXP : KXP + 2 * HX + 1] = np.concatenate([-np.sin(ang), np.cos(ang)], 1)
    hi, lo = split_table(second)
    t2 = np.concatenate(
        [np.concatenate([hi, hi], 1), np.concatenate([lo, np.zeros_like(lo)], 1)], 0
    )
    kz = np.arange(HZ + 1)
    ang = 2.0 * np.pi * ((kz[:, None] * np.arange(GZ)[None, :]) % GZ) / GZ
    third = np.zeros((2 * KZP, GZ))
    third[: HZ + 1] = np.cos(ang)
    third[KZP : KZP + HZ + 1] = np.sin(ang)
    hi, lo = split_table(third)
    t3 = np.concatenate(
        [np.concatenate([hi, hi], 1), np.concatenate([lo, np.zeros_like(lo)], 1)], 0
    )
    perm = np.zeros((LANES, LANES))
    for sub in range(8):
        for rp in range(2 * GROUP):
            perm[sub * 2 * GROUP + rp, rp * 8 + sub] = 1.0
    return t1, t2, t3, perm.astype(ml_dtypes.bfloat16)


def split_value(value):
    hi = value.astype(jnp.bfloat16)
    lo = (value - hi.astype(jnp.float32)).astype(jnp.bfloat16)
    return hi, lo


NN = (((1,), (0,)), ((), ()))
NT = (((1,), (1,)), ((), ()))


def mm(a, b, dims):
    return lax.dot_general(a, b, dims, preferred_element_type=jnp.float32)


def elements_kernel(
    row_blocks,
    col_blocks,
    num_gvec,
    val_rows,
    cond_rows,
    where_row,
    val_ref,
    cond_ref,
    t1_ref,
    t2_ref,
    t3_ref,
    perm_ref,
    scale_ref,
    gvec_ref,
    rows_ref,
    cols_ref,
    uval,
    ucond,
    first,
    second,
    spectrum,
    picked,
):
    step = pl.program_id(0)

    def unpack(i, carry):
        for j in range(64):
            at = i * 64 + j
            columns = pl.ds(pl.multiple_of(at * LANES, LANES), LANES)
            rows = pl.ds(at, BANDS, stride=SPAN)
            uval[rows, :] = val_ref[:, columns].astype(jnp.float32)
            ucond[rows, :] = cond_ref[:, columns].astype(jnp.float32)
        return carry

    lax.fori_loop(0, XCH * GY // 64, unpack, 0)

    def pair_first(p, carry):
        vb = val_rows[p]
        cb = cond_rows[p]
        for half in range(XCH // 2):
            parts = []
            for x in (2 * half, 2 * half + 1):
                base = x * GY
                density = (
                    uval[pl.ds(pl.multiple_of(vb * SPAN + base, 8), GY), :]
                    * ucond[pl.ds(pl.multiple_of(cb * SPAN + base, 8), GY), :]
                )
                hi, lo = split_value(density)
                parts.append(jnp.concatenate([hi, lo], axis=0))
            out = mm(t1_ref[...], jnp.concatenate(parts, axis=1), NN)
            out = out[:ROWS1] + out[ROWS1:]
            for k in range(2):
                at = (p * GX + step * XCH + 2 * half + k) * ROWS1
                first[pl.ds(pl.multiple_of(at, 8), ROWS1), :] = out[:, k * LANES : (k + 1) * LANES]
        return carry

    lax.fori_loop(0, PAIR_DEV, pair_first, 0, unroll=8)

    @pl.when(step == STEPS - 1)
    def _():
        def second_stage(ky, carry):
            for duo in range(PAIR_DEV // 2):
                parts = []
                for p in (2 * duo, 2 * duo + 1):
                    base = p * GX * ROWS1
                    real = first[pl.ds(base + ky, GX, stride=ROWS1), :]
                    imag = first[pl.ds(base + NKY + ky, GX, stride=ROWS1), :]
                    rhi, rlo = split_value(real)
                    ihi, ilo = split_value(imag)
                    parts.append(jnp.concatenate([rhi, ihi, rlo, ilo], axis=0))
                out = mm(t2_ref[...], jnp.concatenate(parts, axis=1), NN)
                out = out[: 2 * KXP] + out[2 * KXP :]
                for k in range(2):
                    for o in range(OCTS):
                        for ri in range(2):
                            group, p = divmod(2 * duo + k, GROUP)
                            at = (ky * OCTS + o) * GROUPS + group
                            at = at * LANES + (ri * GROUP + p) * 8
                            second[pl.ds(pl.multiple_of(at, 8), 8), :] = out[
                                ri * KXP + o * 8 : ri * KXP + o * 8 + 8,
                                k * LANES : (k + 1) * LANES,
                            ]
            return carry

        lax.fori_loop(0, NKY, second_stage, 0, unroll=17)

        lane = lax.broadcasted_iota(jnp.int32, (1, GROUPS * LANES), 1) % LANES
        scale = scale_ref[...]
        swapped = jnp.where(lane < LANES // 2, scale, -scale)

        def third_stage(b, carry):
            value = second[pl.ds(pl.multiple_of(b * 2 * LANES, 2 * LANES), 2 * LANES), :]
            hi, lo = split_value(value)
            out = mm(t3_ref[...], jnp.concatenate([hi, lo], axis=1), NT)
            out = out[: 2 * KZP] + out[2 * KZP :]
            cos_part = out[:KZP] * scale
            sin_part = jnp.concatenate(
                [
                    pltpu.roll(out[KZP:, k * LANES : (k + 1) * LANES], LANES // 2, 1)
                    for k in range(GROUPS)
                ],
                axis=1,
            )
            sin_part = sin_part * swapped
            at = b * 2 * KZP
            plus = cos_part + sin_part
            minus = cos_part - sin_part
            for k in range(GROUPS):
                part = slice(k * LANES, (k + 1) * LANES)
                spectrum[k, pl.ds(pl.multiple_of(at, 8), KZP), :] = plus[:, part]
                spectrum[k, pl.ds(pl.multiple_of(at + KZP, 8), KZP), :] = minus[:, part]
            return carry

        lax.fori_loop(0, SLOTS, third_stage, 0, unroll=17)

        block = num_gvec // col_blocks
        per_row = col_blocks // row_blocks

        for b in range(col_blocks):

            def pick(i, carry):
                sublane = lax.broadcasted_iota(jnp.int32, (8, LANES), 0)
                for j in range(0, 64, 8):
                    at = pl.multiple_of(i * 64 + j, 8)
                    rows = [where_row[b * block + at + n] for n in range(8)]
                    for k in range(GROUPS):
                        tile = jnp.broadcast_to(spectrum[k, pl.ds(rows[0], 1), :], (8, LANES))
                        for n in range(1, 8):
                            line = jnp.broadcast_to(spectrum[k, pl.ds(rows[n], 1), :], (8, LANES))
                            tile = jnp.where(sublane == n, line, tile)
                        picked[k, pl.ds(at, 8), :] = tile
                return carry

            lax.fori_loop(0, block // 64, pick, 0)
            kx, _, _, flip = signed_parts(gvec_ref[:, b * block : (b + 1) * block])
            sub = kx & 7
            sign = flip.astype(jnp.float32)
            real, imag = [], []
            for k in range(GROUPS):
                part = picked[k].astype(jnp.bfloat16)
                turned = mm(perm_ref[...], part, NT)
                total = turned[: 2 * GROUP]
                for s in range(1, 8):
                    total = jnp.where(sub == s, turned[s * 2 * GROUP : (s + 1) * 2 * GROUP], total)
                real.append(total[:GROUP])
                imag.append(total[GROUP:] * sign)
            total = jnp.concatenate(real + imag, axis=0).astype(jnp.bfloat16)
            cols_ref[b] = total
            rows_ref[b // per_row, :, (b % per_row) * block : (b % per_row + 1) * block] = total


def signed_parts(gvec):
    kx = gvec >> 13
    ky = (gvec >> 7) & (GY - 1)
    kz = gvec & (GZ - 1)
    kx = jnp.where(kx < GX // 2, kx, kx - GX)
    ky = jnp.where(ky < GY // 2, ky, ky - GY)
    kz = jnp.where(kz < GZ // 2, kz, kz - GZ)
    flip = jnp.where(ky < 0, -1, 1)
    return kx * flip + HX, ky * flip, kz * flip, flip


def pair_elements(val_rows, cond_rows, scale, val, cond, gvec, row_blocks, col_blocks):
    num_gvec = gvec.shape[0]
    kx, ky, kz, _ = signed_parts(gvec)
    where_row = (ky * OCTS + (kx >> 3)) * 2 * KZP + jnp.where(kz < 0, KZP - kz, kz)
    lanes = jnp.repeat(scale, 8).reshape(GROUPS, 1, -1)
    lanes = jnp.tile(lanes, (1, 2, 1)).reshape(1, -1)
    t1, t2, t3, perm = tables()
    whole = lambda shape: pl.BlockSpec(shape, lambda i, *_: (0,) * len(shape))
    width = XCH * GY * GZ
    outs = [
        jax.ShapeDtypeStruct((row_blocks, 2 * PAIR_DEV, num_gvec // row_blocks), jnp.bfloat16),
        jax.ShapeDtypeStruct((col_blocks, 2 * PAIR_DEV, num_gvec // col_blocks), jnp.bfloat16),
    ]
    return pl.pallas_call(
        functools.partial(elements_kernel, row_blocks, col_blocks, num_gvec),
        out_shape=outs,
        grid_spec=pltpu.PrefetchScalarGridSpec(
            num_scalar_prefetch=3,
            grid=(STEPS,),
            in_specs=[
                pl.BlockSpec((BANDS, width), lambda i, *_: (0, i)),
                pl.BlockSpec((BANDS, width), lambda i, *_: (0, i)),
                whole(t1.shape),
                whole(t2.shape),
                whole(t3.shape),
                whole(perm.shape),
                whole((1, GROUPS * LANES)),
                whole((1, num_gvec)),
            ],
            out_specs=[whole(o.shape) for o in outs],
            scratch_shapes=[
                pltpu.VMEM((SPAN * BANDS, LANES), jnp.float32),
                pltpu.VMEM((SPAN * BANDS, LANES), jnp.float32),
                pltpu.VMEM((PAIR_DEV * GX * ROWS1, LANES), jnp.float32),
                pltpu.VMEM((SLOTS * GROUPS * LANES, LANES), jnp.float32),
                pltpu.VMEM((GROUPS, SLOTS * 2 * KZP, LANES), jnp.float32),
                pltpu.VMEM((GROUPS, num_gvec // col_blocks, LANES), jnp.float32),
            ],
        ),
        compiler_params=pltpu.CompilerParams(vmem_limit_bytes=60 * 1024 * 1024),
    )(val_rows, cond_rows, where_row, val, cond, t1, t2, t3, perm, lanes, gvec[None, :])


def product_kernel(pairs, chunk_row, chunk_col, *refs):
    lefts, rights, before = refs[: len(LEFT)], refs[len(LEFT) : COUNT], refs[COUNT:-4]
    real_ref, imag_ref, lhs, table = refs[-4:]
    width = rights[0].shape[2]
    rows = 2 * PAIR_DEV

    @pl.when(pl.program_id(0) == 0)
    def _():
        for at, (i, k) in enumerate(pairs):
            value = rights[k][chunk_col[i]]
            first = slice(at * rows, at * rows + PAIR_DEV)
            last = slice(at * rows + PAIR_DEV, (at + 1) * rows)
            table[first, :width] = -value[:PAIR_DEV]
            table[last, :width] = -value[PAIR_DEV:]
            table[first, width:] = value[PAIR_DEV:]
            table[last, width:] = -value[:PAIR_DEV]

    for at, (i, k) in enumerate(pairs):
        lhs[at * rows : (at + 1) * rows, :] = lefts[i][chunk_row[k]]
    out = mm(lhs[...], table[...], (((0,), (0,)), ((), ())))
    real, imag = out[:, :width], out[:, width:]
    if before:
        real += before[0][...]
        imag += before[1][...]
    real_ref[...] = real
    imag_ref[...] = imag


HALF = [(0, 0), (0, 1), (-1, 0), (1, 0), (-1, 1), (1, 1), (2, 0), (2, 1)]
LEFT = [(dz, dx, core) for core in range(2) for dz, dx in HALF]
RIGHT = [(dx, dy) for dy, dx in HALF]
COUNT = len(LEFT) + len(RIGHT)
TILE = 256


def panel_product(lefts, rights, pairs, before=()):
    row, col = lax.axis_index("row"), lax.axis_index("col")
    chunk_col = jnp.stack(
        [(col // 4 + dz) % 4 * 4 + (col // 2 % 2 ^ dx) * 2 + (col % 2 ^ dc) for dz, dx, dc in LEFT]
    )
    chunk_row = jnp.stack([(row // 4 ^ dx) * 4 + (row % 4 + dy) % 4 for dx, dy in RIGHT])
    left_at, right_at = sorted({i for i, _ in pairs}), sorted({k for _, k in pairs})
    sources, rows, height = lefts[0].shape
    width = rights[0].shape[2]
    depth = len(pairs) * rows
    out = jax.ShapeDtypeStruct((height, width), jnp.float32)
    out_spec = pl.BlockSpec((TILE, width), lambda m, *_: (m, 0))

    def kernel(chunk_row, chunk_col, *refs):
        left_refs = dict(zip(left_at, refs))
        refs = refs[len(left_at) :]
        right_refs = dict(zip(right_at, refs))
        refs = refs[len(right_at) :]
        all_left = [left_refs.get(i) for i in range(len(LEFT))]
        all_right = [right_refs.get(k) for k in range(len(RIGHT))]
        product_kernel(pairs, chunk_row, chunk_col, *all_left, *all_right, *refs)

    return pl.pallas_call(
        kernel,
        out_shape=[out, out],
        grid_spec=pltpu.PrefetchScalarGridSpec(
            num_scalar_prefetch=2,
            grid=(height // TILE,),
            in_specs=[pl.BlockSpec((sources, rows, TILE), lambda m, *_: (0, 0, m))] * len(left_at)
            + [pl.BlockSpec(rights[0].shape, lambda m, *_: (0, 0, 0))] * len(right_at)
            + [out_spec] * len(before),
            out_specs=[out_spec] * 2,
            scratch_shapes=[
                pltpu.VMEM((depth, TILE), jnp.bfloat16),
                pltpu.VMEM((depth, 2 * width), jnp.bfloat16),
            ],
        ),
        compiler_params=pltpu.CompilerParams(vmem_limit_bytes=60 * 1024 * 1024),
    )(
        chunk_row,
        chunk_col,
        *[lefts[i] for i in left_at],
        *[rights[k] for k in right_at],
        *before,
    )


def ring_z(step):
    return [(c, (c // 4 + step) % 4 * 4 + c % 4) for c in range(16)]


def ring_y(step):
    return [(r, r // 4 * 4 + (r + step) % 4) for r in range(8)]


def pick_values(indices, values):
    match = indices[:, None] == jnp.arange(values.shape[0], dtype=jnp.int32)[None, :]
    return jnp.sum(jnp.where(match, values[None, :], 0.0), axis=1)


def local(val_band, cond_band, val_orbitals, cond_orbitals, val_energy, cond_energy, gvec_index):
    row_count = lax.axis_size("row")
    col_count = lax.axis_size("col")
    pair_dev = val_band.shape[0]
    pairs_all = pair_dev * row_count * col_count
    energy_gap = pick_values(cond_band, cond_energy) - pick_values(val_band, val_energy)
    factor = 4.0 / (math.sqrt(pairs_all) * energy_gap)
    scale = jnp.sqrt(factor) / math.sqrt(GX * GY * GZ)
    val_rows = val_band % val_orbitals.shape[0]
    cond_rows = cond_band % cond_orbitals.shape[0]
    rows_part, cols_part = pair_elements(
        val_rows, cond_rows, scale, val_orbitals, cond_orbitals, gvec_index, row_count, col_count
    )
    swap_core = [(c, c ^ 1) for c in range(col_count)]
    swap_low = [(c, c ^ 2) for c in range(col_count)]
    swap_high = [(r, r ^ 4) for r in range(row_count)]
    along_z = lambda value, step: lax.ppermute(value, "col", ring_z(step))
    along_y = lambda value, step: lax.ppermute(value, "row", ring_y(step))
    cross = lambda value: lax.ppermute(value, "col", swap_core)
    fence = lax.optimization_barrier

    left = [lax.all_to_all(rows_part, "row", split_axis=0, concat_axis=0, tiled=True)]
    cols_part, left = fence((cols_part, left))
    low = lax.ppermute(left[0], "col", swap_low)
    left_near = [along_z(left[0], 1), along_z(left[0], -1)]
    right = [lax.all_to_all(cols_part, "col", split_axis=0, concat_axis=0, tiled=True)]
    left, right = fence((left + [low] + left_near, right))
    left_far = [along_z(left[1], 1), along_z(left[1], -1)]
    right_near = [along_y(right[0], 1), along_y(right[0], -1)]
    high = lax.ppermute(right[0], "row", swap_high)
    left, right = fence((left + left_far, right + [high] + right_near))
    right_far = [along_y(right[1], 1), along_y(right[1], -1)]
    left_ends = [along_z(left[2], 1), along_z(left[5], -1)]
    crossed = [cross(value) for value in left[:4]]
    left, right, crossed = fence((left + left_ends, right + right_far, crossed))
    right_ends = [along_y(right[2], 1), along_y(right[5], -1)]
    crossed_last = [cross(value) for value in left[4:]]
    early = [(i, k) for i in range(12) for k in range(6)]
    late = [(i, k) for i in range(16) for k in range(8) if (i, k) not in early]
    partial = panel_product(left + crossed, right, early)
    real, imag = panel_product(left + crossed + crossed_last, right + right_ends, late, partial)
    return (real, imag)


def solution(mesh):
    return jax.shard_map(
        local,
        mesh=mesh,
        in_specs=(
            P(("row", "col")),
            P(("row", "col")),
            P(("row", "col"), None),
            P(("row", "col"), None),
            P(),
            P(),
            P(),
        ),
        out_specs=(P("row", "col"), P("row", "col")),
        check_vma=False,
    )
```

```python
import functools
import math

import jax
import jax.numpy as jnp
import ml_dtypes
import numpy as np
from jax import lax
from jax.experimental import pallas as pl
from jax.experimental.pallas import tpu as pltpu
from jax.sharding import PartitionSpec as P

GX, GY, GZ = 64, 64, 128
HX, HZ = 16, 32
BANDS = 8
GROUP = 8
GROUPS = 2
PAIR_DEV = GROUP * GROUPS
NKY = HX + 1
ROWS1 = 40
KXP = 40
OCTS = KXP // 8
KZP = 40
SLOTS = NKY * OCTS
XCH = 16
STEPS = GX // XCH
SPAN = XCH * GY + 8
LANES = 128


def split_table(table):
    hi = table.astype(ml_dtypes.bfloat16)
    lo = (table - hi.astype(np.float64)).astype(ml_dtypes.bfloat16)
    return hi, lo


def tables():
    ky = np.arange(NKY)
    ang = 2.0 * np.pi * ((ky[:, None] * np.arange(GY)[None, :]) % GY) / GY
    first = np.zeros((ROWS1, GY))
    first[:NKY] = np.cos(ang)
    first[NKY : 2 * NKY] = -np.sin(ang)
    hi, lo = split_table(first)
    t1 = np.concatenate(
        [np.concatenate([hi, hi], 1), np.concatenate([lo, np.zeros_like(lo)], 1)], 0
    )
    kx = np.arange(2 * HX + 1) - HX
    ang = 2.0 * np.pi * ((kx[:, None] * np.arange(GX)[None, :]) % GX) / GX
    second = np.zeros((2 * KXP, 2 * GX))
    second[: 2 * HX + 1] = np.concatenate([np.cos(ang), np.sin(ang)], 1)
    second[KXP : KXP + 2 * HX + 1] = np.concatenate([-np.sin(ang), np.cos(ang)], 1)
    hi, lo = split_table(second)
    t2 = np.concatenate(
        [np.concatenate([hi, hi], 1), np.concatenate([lo, np.zeros_like(lo)], 1)], 0
    )
    kz = np.arange(HZ + 1)
    ang = 2.0 * np.pi * ((kz[:, None] * np.arange(GZ)[None, :]) % GZ) / GZ
    third = np.zeros((2 * KZP, GZ))
    third[: HZ + 1] = np.cos(ang)
    third[KZP : KZP + HZ + 1] = np.sin(ang)
    hi, lo = split_table(third)
    t3 = np.concatenate(
        [np.concatenate([hi, hi], 1), np.concatenate([lo, np.zeros_like(lo)], 1)], 0
    )
    perm = np.zeros((LANES, LANES))
    for sub in range(8):
        for rp in range(2 * GROUP):
            perm[sub * 2 * GROUP + rp, rp * 8 + sub] = 1.0
    return t1, t2, t3, perm.astype(ml_dtypes.bfloat16)


def split_value(value):
    hi = value.astype(jnp.bfloat16)
    lo = (value - hi.astype(jnp.float32)).astype(jnp.bfloat16)
    return hi, lo


NN = (((1,), (0,)), ((), ()))
NT = (((1,), (1,)), ((), ()))


def mm(a, b, dims):
    return lax.dot_general(a, b, dims, preferred_element_type=jnp.float32)


def elements_kernel(
    row_blocks,
    col_blocks,
    num_gvec,
    pairs_all,
    val_band,
    cond_band,
    where_row,
    val_ref,
    cond_ref,
    t1_ref,
    t2_ref,
    t3_ref,
    perm_ref,
    val_energy,
    cond_energy,
    gvec_ref,
    rows_ref,
    cols_ref,
    uval,
    ucond,
    first,
    second,
    spectrum,
    picked,
):
    step = pl.program_id(0)

    def unpack(i, carry):
        for j in range(64):
            at = i * 64 + j
            columns = pl.ds(pl.multiple_of(at * LANES, LANES), LANES)
            rows = pl.ds(at, BANDS, stride=SPAN)
            uval[rows, :] = val_ref[:, columns].astype(jnp.float32)
            ucond[rows, :] = cond_ref[:, columns].astype(jnp.float32)
        return carry

    lax.fori_loop(0, XCH * GY // 64, unpack, 0)

    def pair_first(p, carry):
        vb = val_band[p] & (BANDS - 1)
        cb = cond_band[p] & (BANDS - 1)
        for half in range(XCH // 2):
            parts = []
            for x in (2 * half, 2 * half + 1):
                base = x * GY
                density = (
                    uval[pl.ds(pl.multiple_of(vb * SPAN + base, 8), GY), :]
                    * ucond[pl.ds(pl.multiple_of(cb * SPAN + base, 8), GY), :]
                )
                hi, lo = split_value(density)
                parts.append(jnp.concatenate([hi, lo], axis=0))
            out = mm(t1_ref[...], jnp.concatenate(parts, axis=1), NN)
            out = out[:ROWS1] + out[ROWS1:]
            for k in range(2):
                at = (p * GX + step * XCH + 2 * half + k) * ROWS1
                first[pl.ds(pl.multiple_of(at, 8), ROWS1), :] = out[:, k * LANES : (k + 1) * LANES]
        return carry

    lax.fori_loop(0, PAIR_DEV, pair_first, 0, unroll=8)

    @pl.when(step == STEPS - 1)
    def _():
        def second_stage(ky, carry):
            for duo in range(PAIR_DEV // 2):
                parts = []
                for p in (2 * duo, 2 * duo + 1):
                    base = p * GX * ROWS1
                    real = first[pl.ds(base + ky, GX, stride=ROWS1), :]
                    imag = first[pl.ds(base + NKY + ky, GX, stride=ROWS1), :]
                    rhi, rlo = split_value(real)
                    ihi, ilo = split_value(imag)
                    parts.append(jnp.concatenate([rhi, ihi, rlo, ilo], axis=0))
                out = mm(t2_ref[...], jnp.concatenate(parts, axis=1), NN)
                out = out[: 2 * KXP] + out[2 * KXP :]
                for k in range(2):
                    for o in range(OCTS):
                        for ri in range(2):
                            group, p = divmod(2 * duo + k, GROUP)
                            at = (ky * OCTS + o) * GROUPS + group
                            at = at * LANES + (ri * GROUP + p) * 8
                            second[pl.ds(pl.multiple_of(at, 8), 8), :] = out[
                                ri * KXP + o * 8 : ri * KXP + o * 8 + 8,
                                k * LANES : (k + 1) * LANES,
                            ]
            return carry

        lax.fori_loop(0, NKY, second_stage, 0, unroll=17)

        lane = lax.broadcasted_iota(jnp.int32, (1, GROUPS * LANES), 1) % LANES
        every = lax.broadcasted_iota(jnp.int32, val_energy.shape, 1)
        place = lax.broadcasted_iota(jnp.int32, (1, GROUPS * LANES), 1)
        owner = (place >> 7) * GROUP + ((place & (LANES // 2 - 1)) >> 3)
        gap = jnp.ones((1, GROUPS * LANES), jnp.float32)
        for p in range(PAIR_DEV):
            upper = jnp.where(every == cond_band[p], cond_energy[...], 0.0)
            lower = jnp.where(every == val_band[p], val_energy[...], 0.0)
            found = jnp.sum(upper - lower, axis=1, keepdims=True)
            gap = jnp.where(owner == p, found, gap)
        factor = 4.0 / (math.sqrt(pairs_all) * gap)
        scale = jnp.sqrt(factor) * (1.0 / math.sqrt(GX * GY * GZ))
        swapped = jnp.where(lane < LANES // 2, scale, -scale)

        def third_stage(b, carry):
            value = second[pl.ds(pl.multiple_of(b * 2 * LANES, 2 * LANES), 2 * LANES), :]
            hi, lo = split_value(value)
            out = mm(t3_ref[...], jnp.concatenate([hi, lo], axis=1), NT)
            out = out[: 2 * KZP] + out[2 * KZP :]
            cos_part = out[:KZP] * scale
            sin_part = jnp.concatenate(
                [
                    pltpu.roll(out[KZP:, k * LANES : (k + 1) * LANES], LANES // 2, 1)
                    for k in range(GROUPS)
                ],
                axis=1,
            )
            sin_part = sin_part * swapped
            at = b * 2 * KZP
            plus = cos_part + sin_part
            minus = cos_part - sin_part
            for k in range(GROUPS):
                part = slice(k * LANES, (k + 1) * LANES)
                spectrum[k, pl.ds(pl.multiple_of(at, 8), KZP), :] = plus[:, part]
                spectrum[k, pl.ds(pl.multiple_of(at + KZP, 8), KZP), :] = minus[:, part]
            return carry

        lax.fori_loop(0, SLOTS, third_stage, 0, unroll=17)

        block = num_gvec // col_blocks
        per_row = col_blocks // row_blocks

        for b in range(col_blocks):

            def pick(i, carry):
                sublane = lax.broadcasted_iota(jnp.int32, (8, LANES), 0)
                for j in range(0, 64, 8):
                    at = pl.multiple_of(i * 64 + j, 8)
                    rows = [where_row[b * block + at + n] for n in range(8)]
                    for k in range(GROUPS):
                        tile = jnp.broadcast_to(spectrum[k, pl.ds(rows[0], 1), :], (8, LANES))
                        for n in range(1, 8):
                            line = jnp.broadcast_to(spectrum[k, pl.ds(rows[n], 1), :], (8, LANES))
                            tile = jnp.where(sublane == n, line, tile)
                        picked[k, pl.ds(at, 8), :] = tile
                return carry

            lax.fori_loop(0, block // 64, pick, 0)
            kx, _, _, flip = signed_parts(gvec_ref[:, b * block : (b + 1) * block])
            sub = kx & 7
            sign = flip.astype(jnp.float32)
            real, imag = [], []
            for k in range(GROUPS):
                part = picked[k].astype(jnp.bfloat16)
                turned = mm(perm_ref[...], part, NT)
                total = turned[: 2 * GROUP]
                for s in range(1, 8):
                    total = jnp.where(sub == s, turned[s * 2 * GROUP : (s + 1) * 2 * GROUP], total)
                real.append(total[:GROUP])
                imag.append(total[GROUP:] * sign)
            total = jnp.concatenate(real + imag, axis=0).astype(jnp.bfloat16)
            cols_ref[b] = total
            rows_ref[b // per_row, :, (b % per_row) * block : (b % per_row + 1) * block] = total


def signed_parts(gvec):
    kx = gvec >> 13
    ky = (gvec >> 7) & (GY - 1)
    kz = gvec & (GZ - 1)
    kx = jnp.where(kx < GX // 2, kx, kx - GX)
    ky = jnp.where(ky < GY // 2, ky, ky - GY)
    kz = jnp.where(kz < GZ // 2, kz, kz - GZ)
    flip = jnp.where(ky < 0, -1, 1)
    return kx * flip + HX, ky * flip, kz * flip, flip


def pair_elements(
    val_band, cond_band, val, cond, val_energy, cond_energy, gvec, row_blocks, col_blocks
):
    pairs_all = val_band.shape[0] * row_blocks * col_blocks
    num_gvec = gvec.shape[0]
    kx, ky, kz, _ = signed_parts(gvec)
    where_row = (ky * OCTS + (kx >> 3)) * 2 * KZP + jnp.where(kz < 0, KZP - kz, kz)
    t1, t2, t3, perm = tables()
    whole = lambda shape: pl.BlockSpec(shape, lambda i, *_: (0,) * len(shape))
    width = XCH * GY * GZ
    outs = [
        jax.ShapeDtypeStruct((row_blocks, 2 * PAIR_DEV, num_gvec // row_blocks), jnp.bfloat16),
        jax.ShapeDtypeStruct((col_blocks, 2 * PAIR_DEV, num_gvec // col_blocks), jnp.bfloat16),
    ]
    return pl.pallas_call(
        functools.partial(elements_kernel, row_blocks, col_blocks, num_gvec, pairs_all),
        out_shape=outs,
        grid_spec=pltpu.PrefetchScalarGridSpec(
            num_scalar_prefetch=3,
            grid=(STEPS,),
            in_specs=[
                pl.BlockSpec((BANDS, width), lambda i, *_: (0, i)),
                pl.BlockSpec((BANDS, width), lambda i, *_: (0, i)),
                whole(t1.shape),
                whole(t2.shape),
                whole(t3.shape),
                whole(perm.shape),
                whole((1, val_energy.shape[0])),
                whole((1, cond_energy.shape[0])),
                whole((1, num_gvec)),
            ],
            out_specs=[whole(o.shape) for o in outs],
            scratch_shapes=[
                pltpu.VMEM((SPAN * BANDS, LANES), jnp.float32),
                pltpu.VMEM((SPAN * BANDS, LANES), jnp.float32),
                pltpu.VMEM((PAIR_DEV * GX * ROWS1, LANES), jnp.float32),
                pltpu.VMEM((SLOTS * GROUPS * LANES, LANES), jnp.float32),
                pltpu.VMEM((GROUPS, SLOTS * 2 * KZP, LANES), jnp.float32),
                pltpu.VMEM((GROUPS, num_gvec // col_blocks, LANES), jnp.float32),
            ],
        ),
        compiler_params=pltpu.CompilerParams(vmem_limit_bytes=60 * 1024 * 1024),
    )(
        val_band,
        cond_band,
        where_row,
        val,
        cond,
        t1,
        t2,
        t3,
        perm,
        val_energy[None, :],
        cond_energy[None, :],
        gvec[None, :],
    )


def product_kernel(pairs, chunk_row, chunk_col, lefts, rights, width, *refs):
    before = refs[:-4]
    real_ref, imag_ref, lhs, table = refs[-4:]
    rows = 2 * PAIR_DEV

    @pl.when(pl.program_id(0) == 0)
    def _():
        for at, (i, k) in enumerate(pairs):
            value = rights(k, i, chunk_col)
            first = slice(at * rows, at * rows + PAIR_DEV)
            last = slice(at * rows + PAIR_DEV, (at + 1) * rows)
            table[first, :width] = -value[:PAIR_DEV]
            table[last, :width] = -value[PAIR_DEV:]
            table[first, width:] = value[PAIR_DEV:]
            table[last, width:] = -value[:PAIR_DEV]

    for at, (i, k) in enumerate(pairs):
        lhs[at * rows : (at + 1) * rows, :] = lefts(i, k, chunk_row)
    out = mm(lhs[...], table[...], (((0,), (0,)), ((), ())))
    real, imag = out[:, :width], out[:, width:]
    if before:
        real += before[0][...]
        imag += before[1][...]
    real_ref[...] = real
    imag_ref[...] = imag


HALF = [(0, 0), (0, 1), (-1, 0), (1, 0), (-1, 1), (1, 1), (2, 0), (2, 1)]
LEFT = [(dz, dx, core) for core in range(2) for dz, dx in HALF]
RIGHT = [(dx, dy) for dy, dx in HALF]
FEW = 2


def panel_product(lefts, rights, pairs, tile, before=()):
    row, col = lax.axis_index("row"), lax.axis_index("col")
    chunk_col = jnp.stack(
        [(col // 4 + dz) % 4 * 4 + (col // 2 % 2 ^ dx) * 2 + (col % 2 ^ dc) for dz, dx, dc in LEFT]
    )
    chunk_row = jnp.stack([(row // 4 ^ dx) * 4 + (row % 4 + dy) % 4 for dx, dy in RIGHT])
    sources, rows, height = lefts[0].shape
    width = rights[0].shape[2]
    depth = len(pairs) * rows
    out = jax.ShapeDtypeStruct((height, width), jnp.float32)
    out_spec = pl.BlockSpec((tile, width), lambda m, *_: (m, 0))

    keys, specs = [], []
    for i in sorted({i for i, _ in pairs}):
        used = [k for j, k in pairs if j == i]
        if len(used) > FEW:
            keys.append(("left", i))
            specs.append(pl.BlockSpec((sources, rows, tile), lambda m, *_: (0, 0, m)))
        for k in used if len(used) <= FEW else []:
            keys.append(("left", i, k))
            specs.append(pl.BlockSpec((1, rows, tile), lambda m, at, _, k=k: (at[k], 0, m)))
    for k in sorted({k for _, k in pairs}):
        used = [i for i, j in pairs if j == k]
        if len(used) > 2 * FEW:
            keys.append(("right", k))
            specs.append(pl.BlockSpec(rights[0].shape, lambda m, *_: (0, 0, 0)))
        for i in used if len(used) <= 2 * FEW else []:
            keys.append(("right", k, i))
            specs.append(pl.BlockSpec((1, rows, width), lambda m, _, at, i=i: (at[i], 0, 0)))
    arrays = [(lefts if key[0] == "left" else rights)[key[1]] for key in keys]

    def kernel(chunk_row, chunk_col, *refs):
        held = dict(zip(keys, refs))

        def part(side, chunk, other, at):
            if (side, chunk) in held:
                return held[side, chunk][at[other]]
            return held[side, chunk, other][0]

        product_kernel(
            pairs,
            chunk_row,
            chunk_col,
            functools.partial(part, "left"),
            functools.partial(part, "right"),
            width,
            *refs[len(keys) :],
        )

    return pl.pallas_call(
        kernel,
        out_shape=[out, out],
        grid_spec=pltpu.PrefetchScalarGridSpec(
            num_scalar_prefetch=2,
            grid=(height // tile,),
            in_specs=specs + [out_spec] * len(before),
            out_specs=[out_spec] * 2,
            scratch_shapes=[
                pltpu.VMEM((depth, tile), jnp.bfloat16),
                pltpu.VMEM((depth, 2 * width), jnp.bfloat16),
            ],
        ),
        compiler_params=pltpu.CompilerParams(vmem_limit_bytes=60 * 1024 * 1024),
    )(
        chunk_row,
        chunk_col,
        *arrays,
        *before,
    )


def ring_z(step):
    return [(c, (c // 4 + step) % 4 * 4 + c % 4) for c in range(16)]


def ring_y(step):
    return [(r, r // 4 * 4 + (r + step) % 4) for r in range(8)]


def local(val_band, cond_band, val_orbitals, cond_orbitals, val_energy, cond_energy, gvec_index):
    row_count = lax.axis_size("row")
    col_count = lax.axis_size("col")
    rows_part, cols_part = pair_elements(
        val_band,
        cond_band,
        val_orbitals,
        cond_orbitals,
        val_energy,
        cond_energy,
        gvec_index,
        row_count,
        col_count,
    )
    swap_core = [(c, c ^ 1) for c in range(col_count)]
    swap_low = [(c, c ^ 2) for c in range(col_count)]
    swap_high = [(r, r ^ 4) for r in range(row_count)]
    along_z = lambda value, step: lax.ppermute(value, "col", ring_z(step))
    along_y = lambda value, step: lax.ppermute(value, "row", ring_y(step))
    cross = lambda value: lax.ppermute(value, "col", swap_core)
    fence = lax.optimization_barrier

    left = [lax.all_to_all(rows_part, "row", split_axis=0, concat_axis=0, tiled=True)]
    cols_part, left = fence((cols_part, left))
    low = lax.ppermute(left[0], "col", swap_low)
    left_near = [along_z(left[0], 1), along_z(left[0], -1)]
    right = [lax.all_to_all(cols_part, "col", split_axis=0, concat_axis=0, tiled=True)]
    left, right = fence((left + [low] + left_near, right))
    left_far = [along_z(left[1], 1), along_z(left[1], -1)]
    right_near = [along_y(right[0], 1), along_y(right[0], -1)]
    high = lax.ppermute(right[0], "row", swap_high)
    left, right = fence((left + left_far, right + [high] + right_near))
    right_far = [along_y(right[1], 1), along_y(right[1], -1)]
    left_ends = [along_z(left[2], 1), along_z(left[5], -1)]
    crossed = [cross(value) for value in left[:4]]
    left, right, crossed = fence((left + left_ends, right + right_far, crossed))
    right_ends = [along_y(right[2], 1), along_y(right[5], -1)]
    crossed_last = [cross(value) for value in left[4:]]
    early = [(i, k) for i in range(12) for k in range(6)]
    late = [(i, k) for i in range(16) for k in range(8) if (i, k) not in early]
    partial = panel_product(left + crossed, right, early, 256)
    real, imag = panel_product(left + crossed + crossed_last, right + right_ends, late, 640, partial)
    return (real, imag)


def solution(mesh):
    return jax.shard_map(
        local,
        mesh=mesh,
        in_specs=(
            P(("row", "col")),
            P(("row", "col")),
            P(("row", "col"), None),
            P(("row", "col"), None),
            P(),
            P(),
            P(),
        ),
        out_specs=(P("row", "col"), P("row", "col")),
        check_vma=False,
    )
```
